32 devices in a mesh: scen: 8 (over z, x), fac: 4 (over y, core).
Axes of the slice: x: 2, y: 2, z: 4, core: 2. Of those that a mesh axis runs over, the one named last changes fastest.
Arguments:
- scenario_draws: bfloat16 [8192, 4096], P('scen'), may hold values from -6 to 6
- cholesky: bfloat16 [4096, 4096], P('scen', 'fac'), may hold values from -1.5 to 1.5, as said below
- exposures: bfloat16 [4096, 4096], P('fac'), may hold values from -0.09375 to 0.09375
- drift: float32 [4096], P('fac'), may hold values from -3 to 3
Outputs:
- covariance: float32 [4096, 4096], P('scen', 'fac')
- expected: float32 [4096], P('fac')
The draws below stay inside these ranges and needn't reach their ends.
Inputs may be any that keep to these rules, and one draw needn't show every extreme that they name: cholesky is lower triangular (zero above the diagonal) with diagonal entries of 0.5 to 1.5.
All inputs are finite; a program needn't handle non-finite values.
Results may differ from the reference program's by a relative error of at most 0.0013.
Values may be sent and summed in bfloat16 or wider, within the bound.
A program may use at most 128 MiB of HBM per device.

```python
import jax
import jax.numpy as jnp
from jax import lax

F = 4096
DESKS = 4096
SCEN = 8192


def draw_cholesky(key, part):
    key_low, key_diag = jax.random.split(jax.random.fold_in(key, 7))
    below = jax.random.truncated_normal(key_low, -4.0, 4.0, (F, F), jnp.float32) / jnp.sqrt(jnp.float32(F))
    lower = jnp.tril(below, -1)
    diag_vals = jax.random.uniform(key_diag, (F,), jnp.float32, 0.5, 1.5)
    return (lower + jnp.diag(diag_vals)).astype(jnp.bfloat16)


def shard_levels(key, shape, cuts, smallest, high):
    loudness = 1.0
    for axis_at, blocks in cuts:
        draws = jax.random.uniform(jax.random.fold_in(jax.random.fold_in(key, 6), axis_at), (blocks,), jnp.float32, smallest / len(cuts), high / len(cuts))
        loudness = loudness * jnp.repeat(jnp.exp(draws), shape[axis_at] // blocks).reshape((-1,) + (1,) * (len(shape) - 1 - axis_at))
    return loudness


def normal_values(rng, shape, spread, reach, cuts=(), held_as=jnp.bfloat16):
    gain = shard_levels(rng, shape, cuts, -0.22, 0.18) if cuts else 1.0
    result = jax.random.normal(rng, shape, jnp.float32) * spread * gain
    return jnp.minimum(jnp.maximum(result, -reach), reach).astype(held_as)


def setup_inputs(seed: int = 0) -> dict:
    arg_keys = jax.random.split(jax.random.key(seed), 5)
    return {
        "scenario_draws": normal_values(arg_keys[0], (SCEN, F), 1.0, 6.0, ((0, 8),)),
        "cholesky": draw_cholesky(jax.random.fold_in(arg_keys[4], 71), 0),
        "exposures": normal_values(arg_keys[2], (DESKS, F), F ** -0.5, 0.09375, ((0, 4),)),
        "drift": normal_values(arg_keys[3], (F,), 0.5, 3.0, ((0, 4),), jnp.float32),
    }


def reference(scenario_draws, cholesky, exposures, drift):
    mixed = jnp.dot(scenario_draws, cholesky, preferred_element_type=jnp.float32)
    shocks = (mixed + drift[None, :]).astype(jnp.bfloat16)
    pnl = lax.dot_general(shocks, exposures, (((1,), (1,)), ((), ())), preferred_element_type=jnp.float32).astype(jnp.bfloat16)
    expected = jnp.sum(pnl, axis=0, dtype=jnp.float32) / SCEN
    gram = lax.dot_general(pnl, pnl, (((0,), (0,)), ((), ())), preferred_element_type=jnp.float32)
    covariance = (gram - SCEN * expected[:, None] * expected[None, :]) / (SCEN - 1)
    return covariance, expected
```

```python
import jax
import jax.numpy as jnp
from jax import lax
from jax.sharding import PartitionSpec as P

BF16, F16, F32 = jnp.bfloat16, jnp.float16, jnp.float32
CHUNKS = 2


def flip(size, bit):
    return [(i, i ^ bit) for i in range(size)]


def swap(value, axis, bit):
    return lax.ppermute(value, axis, flip(lax.axis_size(axis), bit))


def rows_dot(a, b):
    return lax.dot_general(a, b, (((0,), (0,)), ((), ())), preferred_element_type=F32)


def cols_dot(a, b):
    return lax.dot_general(a, b, (((1,), (1,)), ((), ())), preferred_element_type=F32)


def on_device(scenario_draws, cholesky, exposures, drift):
    n_scen, n_fac = lax.axis_size("scen"), lax.axis_size("fac")
    si, fi = lax.axis_index("scen"), lax.axis_index("fac")
    nz = n_scen // 2
    zi, xi = si // 2, si % 2
    count = scenario_draws.shape[0]
    own = exposures.shape[0]
    desks = own * n_fac
    block = desks // n_scen
    per_fac = own // block // 2
    factors = cholesky.shape[1]
    total = count * n_scen
    plane = 2 * count

    chol = lax.all_gather(cholesky, "scen", axis=0, tiled=True)
    weights = [
        lax.dynamic_slice_in_dim(exposures, (fi ^ k) * factors, factors, 1) for k in range(n_fac)
    ]

    def own_parity(value):
        split = value.reshape(value.shape[0], per_fac, 2, block)
        return lax.dynamic_index_in_dim(split, xi, 2, keepdims=False).reshape(
            value.shape[0], per_fac * block
        )

    cols, picks = [], [[] for _ in range(n_fac)]
    step = count // CHUNKS
    for c in range(CHUNKS):
        draws = scenario_draws[c * step : (c + 1) * step]
        mixed = jnp.dot(draws, chol, preferred_element_type=F32)
        shocks = (mixed + drift[None, :]).astype(BF16)
        far = swap(shocks, "fac", 2)
        parts = [shocks, swap(shocks, "fac", 1), far, swap(far, "fac", 1)]
        acc = cols_dot(parts[0], weights[0])
        for k in range(1, n_fac):
            acc = acc + cols_dot(parts[k], weights[k])
        pnl = acc.astype(BF16)
        for piece in (pnl, swap(pnl, "scen", 1)):
            cols.append(piece)
            mine = own_parity(piece)
            across = swap(mine, "fac", 2)
            got = [mine, swap(mine, "fac", 1), across, swap(across, "fac", 1)]
            for k in range(n_fac):
                picks[k].append(got[k])

    col = jnp.concatenate(cols, axis=0)
    rows = [jnp.concatenate(p, axis=0) for p in picks]

    col_sum = jnp.sum(col, axis=0, dtype=F32)
    row_sum = jnp.stack([jnp.sum(r, axis=0, dtype=F32) for r in rows])
    col_sq = jnp.max(jnp.sum(jnp.square(col.astype(F32)), axis=0))
    row_sq = jnp.max(jnp.stack([jnp.max(jnp.sum(jnp.square(r.astype(F32)), axis=0)) for r in rows]))
    bound = jnp.sqrt(col_sq) * jnp.sqrt(row_sq) * 1.01

    parts = jnp.stack(
        [
            rows_dot(rows[k], col) - row_sum[k][:, None] * (col_sum / plane)[None, :]
            for k in range(n_fac)
        ]
    ).reshape(n_fac, per_fac, block, own)

    def block_of(array, z):
        z = jnp.clip(z, 0, nz - 1)
        return lax.dynamic_slice(
            array, (fi ^ (z // per_fac), z % per_fac) + (0,) * (array.ndim - 2), (1, 1) + array.shape[2:]
        ).reshape(array.shape[2:])

    row_sums = row_sum.reshape(n_fac, per_fac, block)

    def pack(value, limit):
        safe = jnp.where(limit > 0, limit, 1.0)
        scale = jnp.exp2(jnp.floor(14.0 - jnp.log2(safe)))
        return (value * scale).astype(F16), jnp.full((8, 128), scale), jnp.full((8, 128), limit)

    def unpack(packed):
        code, scale, limit = packed
        return code.astype(F32) / jnp.where(scale[0, 0] > 0, scale[0, 0], 1.0), limit[0, 0]

    mine = block_of(parts, zi)
    for up in (True, False):
        arrived = None
        for t in range(1, nz):
            if up:
                pairs = [(z, z + 1) for z in range(t)]
                target = nz - t + zi
            else:
                pairs = [(nz - 1 - z, nz - 2 - z) for z in range(t)]
                target = zi + t - nz
            pairs = [(2 * a + x, 2 * b + x) for a, b in pairs for x in range(2)]
            value, limit = block_of(parts, target), bound
            if arrived is not None:
                value, limit = value + arrived[0], limit + arrived[1]
            sent = [lax.ppermute(v, "scen", pairs) for v in pack(value, limit)]
            arrived = unpack(sent)
        mine = mine + arrived[0]

    sums = jnp.concatenate([col_sum, row_sums.reshape(-1)])
    groups = [[2 * z + x for z in range(nz)] for x in range(2)]
    all_sums = lax.all_gather(sums, "scen", axis=0, axis_index_groups=groups)
    all_cols = all_sums[:, :own]
    all_rows = jnp.stack(
        [block_of(all_sums[z, own:].reshape(n_fac, per_fac, block), zi) for z in range(nz)]
    )
    col_total = jnp.sum(all_cols, axis=0)
    row_total = jnp.sum(all_rows, axis=0)
    fix = -row_total[:, None] * (col_total / total)[None, :]
    for z in range(nz):
        fix = fix + all_rows[z][:, None] * (all_cols[z] / plane)[None, :]
    return (mine + fix) / (total - 1), col_total / total


def solution(mesh):
    placed = (P("scen", None), P("scen", "fac"), P("fac", None), P("fac"))
    return jax.shard_map(
        on_device,
        mesh=mesh,
        in_specs=placed,
        out_specs=(P("scen", "fac"), P("fac")),
        check_vma=False,
    )
```

```python
import jax
import jax.numpy as jnp
from jax import lax
from jax.sharding import PartitionSpec as P

BF16, F16, F32 = jnp.bfloat16, jnp.float16, jnp.float32
CHUNKS = 2


def flip(size, bit):
    return [(i, i ^ bit) for i in range(size)]


def swap(value, axis, bit):
    return lax.ppermute(value, axis, flip(lax.axis_size(axis), bit))


def rows_dot(a, b):
    return lax.dot_general(a, b, (((0,), (0,)), ((), ())), preferred_element_type=F32)


def cols_dot(a, b):
    return lax.dot_general(a, b, (((1,), (1,)), ((), ())), preferred_element_type=F32)


def on_device(scenario_draws, cholesky, exposures, drift):
    n_scen, n_fac = lax.axis_size("scen"), lax.axis_size("fac")
    si, fi = lax.axis_index("scen"), lax.axis_index("fac")
    nz = n_scen // 2
    zi, xi = si // 2, si % 2
    count = scenario_draws.shape[0]
    own = exposures.shape[0]
    desks = own * n_fac
    block = desks // n_scen
    per_fac = own // block // 2
    factors = cholesky.shape[1]
    total = count * n_scen
    plane = 2 * count

    chol = lax.all_gather(cholesky, "scen", axis=0, tiled=True)
    weights = [
        lax.dynamic_slice_in_dim(exposures, (fi ^ k) * factors, factors, 1) for k in range(n_fac)
    ]

    def own_parity(value):
        split = value.reshape(value.shape[0], per_fac, 2, block)
        return lax.dynamic_index_in_dim(split, xi, 2, keepdims=False).reshape(
            value.shape[0], per_fac * block
        )

    grams = [0.0] * n_fac
    sums, squares = [0.0, 0.0], [0.0, 0.0]
    step = count // CHUNKS
    for c in range(CHUNKS):
        draws = scenario_draws[c * step : (c + 1) * step]
        mixed = jnp.dot(draws, chol, preferred_element_type=F32)
        shocks = (mixed + drift[None, :]).astype(BF16)
        far = swap(shocks, "fac", 2)
        parts = [shocks, swap(shocks, "fac", 1), far, swap(far, "fac", 1)]
        acc = cols_dot(parts[0], weights[0])
        for k in range(1, n_fac):
            acc = acc + cols_dot(parts[k], weights[k])
        pnl = acc.astype(BF16)
        for side, piece in enumerate((pnl, swap(pnl, "scen", 1))):
            wide = piece.astype(F32)
            sums[side] = sums[side] + jnp.sum(wide, axis=0)
            squares[side] = squares[side] + jnp.sum(jnp.square(wide), axis=0)
            mine = own_parity(piece)
            across = swap(mine, "fac", 2)
            got = [mine, swap(mine, "fac", 1), across, swap(across, "fac", 1)]
            for k in range(n_fac):
                grams[k] = grams[k] + rows_dot(got[k], piece)

    largest = jnp.max(squares[0] + squares[1])
    stats = jnp.concatenate([sums[0] + sums[1], jnp.full((128,), largest)])
    around = [stats]
    for k in range(1, nz):
        pairs = [(2 * z + x, 2 * ((z + k) % nz) + x) for z in range(nz) for x in range(2)]
        around.append(lax.ppermute(stats, "scen", pairs))
    around = jnp.stack(around)
    by_z = jnp.stack(
        [
            lax.dynamic_index_in_dim(around, (zi - z + nz) % nz, 0, keepdims=False)
            for z in range(nz)
        ]
    )
    far = swap(by_z, "fac", 2)
    everyone = jnp.stack([by_z, swap(by_z, "fac", 1), far, swap(far, "fac", 1)])
    limit = jnp.max(everyone[:, :, own:]) * (1.01 * nz)
    power = jnp.floor(14.0 - jnp.log2(jnp.where(limit > 0, limit, 1.0)))
    scale = jnp.exp2(jnp.clip(power, -100.0, 100.0))

    col_sums = by_z[:, :own]
    row_sums = own_parity(everyone[:, :, :own].reshape(n_fac * nz, own)).reshape(
        n_fac, nz, per_fac, block
    )
    here = lax.dynamic_index_in_dim(row_sums, zi, 1, keepdims=False)
    col_mean = (sums[0] + sums[1]) / plane

    def block_of(array, z):
        z = jnp.clip(z, 0, nz - 1)
        return lax.dynamic_slice(
            array, (fi ^ (z // per_fac), z % per_fac) + (0,) * (array.ndim - 2), (1, 1) + array.shape[2:]
        ).reshape(array.shape[2:])

    parts = jnp.stack(
        [
            (grams[k] - here[k].reshape(-1)[:, None] * col_mean[None, :]) * scale
            for k in range(n_fac)
        ]
    ).reshape(n_fac, per_fac, block, own)

    mine = block_of(parts, zi)
    arrived = [None, None]
    for t in range(1, nz):
        for up in (0, 1):
            if up:
                pairs = [(z, z + 1) for z in range(t)]
                target = nz - t + zi
            else:
                pairs = [(nz - 1 - z, nz - 2 - z) for z in range(t)]
                target = zi + t - nz
            pairs = [(2 * a + x, 2 * b + x) for a, b in pairs for x in range(2)]
            value = block_of(parts, target)
            if arrived[up] is not None:
                value = value + arrived[up].astype(F32)
            arrived[up] = lax.ppermute(value.astype(F16), "scen", pairs)
    mine = (mine + arrived[0].astype(F32) + arrived[1].astype(F32)) / scale

    my_rows = jnp.stack([block_of(row_sums[:, z], zi) for z in range(nz)])
    col_total = jnp.sum(col_sums, axis=0)
    row_total = jnp.sum(my_rows, axis=0)
    fix = -row_total[:, None] * (col_total / total)[None, :]
    for z in range(nz):
        fix = fix + my_rows[z][:, None] * (col_sums[z] / plane)[None, :]
    return (mine + fix) / (total - 1), col_total / total


def solution(mesh):
    placed = (P("scen", None), P("scen", "fac"), P("fac", None), P("fac"))
    return jax.shard_map(
        on_device,
        mesh=mesh,
        in_specs=placed,
        out_specs=(P("scen", "fac"), P("fac")),
        check_vma=False,
    )
```

```python
import jax
import jax.numpy as jnp
from jax import lax
from jax.sharding import PartitionSpec as P

BF16, F16, F32 = jnp.bfloat16, jnp.float16, jnp.float32
CHUNKS = 2


def flip(size, bit):
    return [(i, i ^ bit) for i in range(size)]


def swap(value, axis, bit):
    return lax.ppermute(value, axis, flip(lax.axis_size(axis), bit))


def rows_dot(a, b):
    return lax.dot_general(a, b, (((0,), (0,)), ((), ())), preferred_element_type=F32)


def cols_dot(a, b):
    return lax.dot_general(a, b, (((1,), (1,)), ((), ())), preferred_element_type=F32)


def on_device(scenario_draws, cholesky, exposures, drift):
    n_scen, n_fac = lax.axis_size("scen"), lax.axis_size("fac")
    si, fi = lax.axis_index("scen"), lax.axis_index("fac")
    nz = n_scen // 2
    zi, xi = si // 2, si % 2
    count = scenario_draws.shape[0]
    own = exposures.shape[0]
    desks = own * n_fac
    block = desks // n_scen
    per_fac = own // block // 2
    factors = cholesky.shape[1]
    total = count * n_scen
    plane = 2 * count

    depth = cholesky.shape[0]

    def along_z(value, pairs):
        return lax.ppermute(
            value, "scen", [(2 * a + x, 2 * b + x) for a, b in pairs for x in range(2)]
        )

    def across_x(value, zs):
        return lax.ppermute(value, "scen", [(2 * z + x, 2 * z + 1 - x) for z in zs for x in range(2)])

    above, below = [cholesky], [cholesky]
    for t in range(1, nz):
        above.append(along_z(above[-1], [(z - 1, z) for z in range(t, nz)]))
        below.append(along_z(below[-1], [(z + 1, z) for z in range(nz - t)]))
    chol = [(si, cholesky), (si ^ 1, swap(cholesky, "scen", 1))]
    far_above = [across_x(above[t], range(t, nz)) for t in range(1, nz)]
    far_below = [across_x(below[t], range(nz - t)) for t in range(1, nz)]
    for t in range(1, nz):
        home = 2 * ((zi - t + nz) % nz) + xi
        chol.append((home, jnp.where(zi >= t, above[t], below[nz - t])))
        chol.append((home ^ 1, jnp.where(zi >= t, far_above[t - 1], far_below[nz - t - 1])))
    lower = jnp.concatenate([piece for _, piece in chol], axis=0)
    turned = jnp.concatenate(
        [lax.dynamic_slice_in_dim(scenario_draws, home * depth, depth, 1) for home, _ in chol], axis=1
    )
    weights = [
        lax.dynamic_slice_in_dim(exposures, (fi ^ k) * factors, factors, 1) for k in range(n_fac)
    ]

    def own_parity(value):
        split = value.reshape(value.shape[0], per_fac, 2, block)
        return lax.dynamic_index_in_dim(split, xi, 2, keepdims=False).reshape(
            value.shape[0], per_fac * block
        )

    grams = [0.0] * n_fac
    sums, squares = [0.0, 0.0], [0.0, 0.0]
    step = count // CHUNKS
    for c in range(CHUNKS):
        draws = turned[c * step : (c + 1) * step]
        mixed = jnp.dot(draws, lower, preferred_element_type=F32)
        shocks = (mixed + drift[None, :]).astype(BF16)
        far = swap(shocks, "fac", 2)
        parts = [shocks, swap(shocks, "fac", 1), far, swap(far, "fac", 1)]
        acc = cols_dot(parts[0], weights[0])
        for k in range(1, n_fac):
            acc = acc + cols_dot(parts[k], weights[k])
        pnl = acc.astype(BF16)
        for side, piece in enumerate((pnl, swap(pnl, "scen", 1))):
            wide = piece.astype(F32)
            sums[side] = sums[side] + jnp.sum(wide, axis=0)
            squares[side] = squares[side] + jnp.sum(jnp.square(wide), axis=0)
            mine = own_parity(piece)
            across = swap(mine, "fac", 2)
            got = [mine, swap(mine, "fac", 1), across, swap(across, "fac", 1)]
            for k in range(n_fac):
                grams[k] = grams[k] + rows_dot(got[k], piece)

    largest = jnp.max(squares[0] + squares[1])
    stats = jnp.concatenate([sums[0] + sums[1], jnp.full((128,), largest)])
    around = [stats]
    for k in range(1, nz):
        pairs = [(2 * z + x, 2 * ((z + k) % nz) + x) for z in range(nz) for x in range(2)]
        around.append(lax.ppermute(stats, "scen", pairs))
    around = jnp.stack(around)
    by_z = jnp.stack(
        [
            lax.dynamic_index_in_dim(around, (zi - z + nz) % nz, 0, keepdims=False)
            for z in range(nz)
        ]
    )
    far = swap(by_z, "fac", 2)
    everyone = jnp.stack([by_z, swap(by_z, "fac", 1), far, swap(far, "fac", 1)])
    limit = jnp.max(everyone[:, :, own:]) * (1.01 * nz)
    power = jnp.floor(14.0 - jnp.log2(jnp.where(limit > 0, limit, 1.0)))
    scale = jnp.exp2(jnp.clip(power, -100.0, 100.0))

    col_sums = by_z[:, :own]
    row_sums = own_parity(everyone[:, :, :own].reshape(n_fac * nz, own)).reshape(
        n_fac, nz, per_fac, block
    )
    here = lax.dynamic_index_in_dim(row_sums, zi, 1, keepdims=False)
    col_mean = (sums[0] + sums[1]) / plane

    def block_of(array, z):
        z = jnp.clip(z, 0, nz - 1)
        return lax.dynamic_slice(
            array, (fi ^ (z // per_fac), z % per_fac) + (0,) * (array.ndim - 2), (1, 1) + array.shape[2:]
        ).reshape(array.shape[2:])

    parts = jnp.stack(
        [
            (grams[k] - here[k].reshape(-1)[:, None] * col_mean[None, :]) * scale
            for k in range(n_fac)
        ]
    ).reshape(n_fac, per_fac, block, own)

    mine = block_of(parts, zi)
    arrived = [None, None]
    for t in range(1, nz):
        for up in (0, 1):
            if up:
                pairs = [(z, z + 1) for z in range(t)]
                target = nz - t + zi
            else:
                pairs = [(nz - 1 - z, nz - 2 - z) for z in range(t)]
                target = zi + t - nz
            pairs = [(2 * a + x, 2 * b + x) for a, b in pairs for x in range(2)]
            value = block_of(parts, target)
            if arrived[up] is not None:
                value = value + arrived[up].astype(F32)
            arrived[up] = lax.ppermute(value.astype(F16), "scen", pairs)
    mine = (mine + arrived[0].astype(F32) + arrived[1].astype(F32)) / scale

    my_rows = jnp.stack([block_of(row_sums[:, z], zi) for z in range(nz)])
    col_total = jnp.sum(col_sums, axis=0)
    row_total = jnp.sum(my_rows, axis=0)
    fix = -row_total[:, None] * (col_total / total)[None, :]
    for z in range(nz):
        fix = fix + my_rows[z][:, None] * (col_sums[z] / plane)[None, :]
    return (mine + fix) / (total - 1), col_total / total


def solution(mesh):
    placed = (P("scen", None), P("scen", "fac"), P("fac", None), P("fac"))
    return jax.shard_map(
        on_device,
        mesh=mesh,
        in_specs=placed,
        out_specs=(P("scen", "fac"), P("fac")),
        check_vma=False,
    )
```

```python
import jax
import jax.numpy as jnp
from jax import lax
from jax.sharding import PartitionSpec as P

BF16, F16, F32 = jnp.bfloat16, jnp.float16, jnp.float32
CHUNKS = 4


def flip(size, bit):
    return [(i, i ^ bit) for i in range(size)]


def swap(value, axis, bit):
    return lax.ppermute(value, axis, flip(lax.axis_size(axis), bit))


def rows_dot(a, b):
    return lax.dot_general(a, b, (((0,), (0,)), ((), ())), preferred_element_type=F32)


def cols_dot(a, b):
    return lax.dot_general(a, b, (((1,), (1,)), ((), ())), preferred_element_type=F32)


def on_device(scenario_draws, cholesky, exposures, drift):
    n_scen, n_fac = lax.axis_size("scen"), lax.axis_size("fac")
    si, fi = lax.axis_index("scen"), lax.axis_index("fac")
    nz = n_scen // 2
    zi, xi = si // 2, si % 2
    count = scenario_draws.shape[0]
    own = exposures.shape[0]
    desks = own * n_fac
    block = desks // n_scen
    per_fac = own // block // 2
    factors = cholesky.shape[1]
    total = count * n_scen
    plane = 2 * count

    depth = cholesky.shape[0]

    def along_z(value, pairs):
        return lax.ppermute(
            value, "scen", [(2 * a + x, 2 * b + x) for a, b in pairs for x in range(2)]
        )

    def across_x(value, zs):
        return lax.ppermute(value, "scen", [(2 * z + x, 2 * z + 1 - x) for z in zs for x in range(2)])

    above, below = [cholesky], [cholesky]
    for t in range(1, nz):
        above.append(along_z(above[-1], [(z - 1, z) for z in range(t, nz)]))
        below.append(along_z(below[-1], [(z + 1, z) for z in range(nz - t)]))
    chol = [(si, cholesky), (si ^ 1, swap(cholesky, "scen", 1))]
    far_above = [across_x(above[t], range(t, nz)) for t in range(1, nz)]
    far_below = [across_x(below[t], range(nz - t)) for t in range(1, nz)]
    for t in range(1, nz):
        home = 2 * ((zi - t + nz) % nz) + xi
        chol.append((home, jnp.where(zi >= t, above[t], below[nz - t])))
        chol.append((home ^ 1, jnp.where(zi >= t, far_above[t - 1], far_below[nz - t - 1])))
    lower = jnp.concatenate([piece for _, piece in chol], axis=0)
    turned = jnp.concatenate(
        [lax.dynamic_slice_in_dim(scenario_draws, home * depth, depth, 1) for home, _ in chol], axis=1
    )
    weights = [
        lax.dynamic_slice_in_dim(exposures, (fi ^ k) * factors, factors, 1) for k in range(n_fac)
    ]

    def own_parity(value):
        split = value.reshape(value.shape[0], per_fac, 2, block)
        return lax.dynamic_index_in_dim(split, xi, 2, keepdims=False).reshape(
            value.shape[0], per_fac * block
        )

    grams = [0.0] * n_fac
    sums, squares = [0.0, 0.0], [0.0, 0.0]
    step = count // CHUNKS
    for c in range(CHUNKS):
        draws = turned[c * step : (c + 1) * step]
        mixed = jnp.dot(draws, lower, preferred_element_type=F32)
        shocks = (mixed + drift[None, :]).astype(BF16)
        far = swap(shocks, "fac", 2)
        parts = [shocks, swap(shocks, "fac", 1), far, swap(far, "fac", 1)]
        acc = cols_dot(parts[0], weights[0])
        for k in range(1, n_fac):
            acc = acc + cols_dot(parts[k], weights[k])
        pnl = acc.astype(BF16)
        for side, piece in enumerate((pnl, swap(pnl, "scen", 1))):
            wide = piece.astype(F32)
            sums[side] = sums[side] + jnp.sum(wide, axis=0)
            squares[side] = squares[side] + jnp.sum(jnp.square(wide), axis=0)
            mine = own_parity(piece)
            across = swap(mine, "fac", 2)
            got = [mine, swap(mine, "fac", 1), across, swap(across, "fac", 1)]
            for k in range(n_fac):
                grams[k] = grams[k] + rows_dot(got[k], piece)

    largest = jnp.max(squares[0] + squares[1])
    stats = jnp.concatenate([sums[0] + sums[1], jnp.full((128,), largest)])
    around = [stats]
    for k in range(1, nz):
        pairs = [(2 * z + x, 2 * ((z + k) % nz) + x) for z in range(nz) for x in range(2)]
        around.append(lax.ppermute(stats, "scen", pairs))
    around = jnp.stack(around)
    by_z = jnp.stack(
        [
            lax.dynamic_index_in_dim(around, (zi - z + nz) % nz, 0, keepdims=False)
            for z in range(nz)
        ]
    )
    far = swap(by_z, "fac", 2)
    everyone = jnp.stack([by_z, swap(by_z, "fac", 1), far, swap(far, "fac", 1)])
    limit = jnp.max(everyone[:, :, own:]) * (1.01 * nz)
    power = jnp.floor(14.0 - jnp.log2(jnp.where(limit > 0, limit, 1.0)))
    scale = jnp.exp2(jnp.clip(power, -100.0, 100.0))

    col_sums = by_z[:, :own]
    row_sums = own_parity(everyone[:, :, :own].reshape(n_fac * nz, own)).reshape(
        n_fac, nz, per_fac, block
    )
    here = lax.dynamic_index_in_dim(row_sums, zi, 1, keepdims=False)
    col_mean = (sums[0] + sums[1]) / plane

    def block_of(array, z):
        z = jnp.clip(z, 0, nz - 1)
        return lax.dynamic_slice(
            array, (fi ^ (z // per_fac), z % per_fac) + (0,) * (array.ndim - 2), (1, 1) + array.shape[2:]
        ).reshape(array.shape[2:])

    parts = jnp.stack(
        [
            (grams[k] - here[k].reshape(-1)[:, None] * col_mean[None, :]) * scale
            for k in range(n_fac)
        ]
    ).reshape(n_fac, per_fac, block, own)

    mine = block_of(parts, zi)
    arrived = [None, None]
    for t in range(1, nz):
        for up in (0, 1):
            if up:
                pairs = [(z, z + 1) for z in range(t)]
                target = nz - t + zi
            else:
                pairs = [(nz - 1 - z, nz - 2 - z) for z in range(t)]
                target = zi + t - nz
            pairs = [(2 * a + x, 2 * b + x) for a, b in pairs for x in range(2)]
            value = block_of(parts, target)
            if arrived[up] is not None:
                value = value + arrived[up].astype(F32)
            arrived[up] = lax.ppermute(value.astype(F16), "scen", pairs)
    mine = (mine + arrived[0].astype(F32) + arrived[1].astype(F32)) / scale

    my_rows = jnp.stack([block_of(row_sums[:, z], zi) for z in range(nz)])
    col_total = jnp.sum(col_sums, axis=0)
    row_total = jnp.sum(my_rows, axis=0)
    fix = -row_total[:, None] * (col_total / total)[None, :]
    for z in range(nz):
        fix = fix + my_rows[z][:, None] * (col_sums[z] / plane)[None, :]
    return (mine + fix) / (total - 1), col_total / total


def solution(mesh):
    placed = (P("scen", None), P("scen", "fac"), P("fac", None), P("fac"))
    return jax.shard_map(
        on_device,
        mesh=mesh,
        in_specs=placed,
        out_specs=(P("scen", "fac"), P("fac")),
        check_vma=False,
    )
```
